256 devices in a mesh: sp: 16 (over z_lo, y, core), tp: 4 (over x), dp: 4 (over z_hi).
Axes of the slice: x: 4, y: 4, z: 8 (z_hi: 4, z_lo: 2; z = z_hi * 2 + z_lo), core: 2. Of those that a mesh axis runs over, the one named last changes fastest.
Arguments:
- queries: bfloat16 [16, 16, 32, 4096], P('dp', 'sp', 'tp'), parts along dimension 0
- key_proj: bfloat16 [16, 16, 32, 4096], P('dp', 'sp', 'tp'), parts along dimension 0
- values: bfloat16 [16, 16, 32, 4096], P('dp', 'sp', 'tp'), parts along dimension 0, may hold values from -6 to 6
- hidden_in: bfloat16 [16, 16, 32, 5120], P('dp', 'sp', 'tp'), parts along dimension 0, may hold values from -6 to 6
- out_weight: bfloat16 [4096, 5120], P('sp', 'tp'), may hold values from -0.09375 to 0.09375
- out_gate: float32 [5120], replicated, may hold values from 0.1 to 1.9
- mod_shift: float32 [5120], replicated, may hold values from -3 to 3
- mod_scale: float32 [5120], replicated, may hold values from -0.5 to 0.5
- head_weight: bfloat16 [5120, 64], replicated, may hold values from -0.078125 to 0.078125
- conv_first: bfloat16 [432, 384], replicated, may hold values from -0.3125 to 0.3125
- bias_first: float32 [384], replicated, may hold values from -3 to 3
- norm_gain: float32 [384], replicated, may hold values from 0.1 to 1.9
- conv_second: bfloat16 [10368, 384], replicated, may hold values from -0.0625 to 0.0625
- bias_second: float32 [384], replicated, may hold values from -3 to 3
Outputs:
- block_out: bfloat16 [16, 16, 32, 5120], P('dp', 'sp', 'tp'), parts along dimension 0
- decoded: bfloat16 [16, 32, 64, 384], P('dp', 'sp', 'tp'), parts along dimension 0
The draws below stay inside these ranges and needn't reach their ends.
There are 4 independent parts, one for each index of `dp`. The reference program is written for one: setup_inputs(seed, part) draws one part's arguments, and reference() takes and returns one part's arrays. A program takes and returns all parts, laid end to end along the dimension named above; an argument that names none is the same for every part. Nothing has to cross between parts.
All inputs are finite; a program needn't handle non-finite values.
Results may differ from the reference program's by a relative error of at most 0.02.
Values may be sent and summed in bfloat16 or wider, within the bound.
No kernel may reach another device: no remote copies, remote signals or barrier semaphores. Data moves between devices by JAX's collectives and lax.ppermute only.
A program may use at most 64 MiB of HBM per device.

```python
import jax
import jax.numpy as jnp
from jax import lax

D = 5120
HEAD_DIM = 128
LAT_CH = 16
VC = 384
HEAD_DEV = 2
FRAMES = 4
HEADS = 32
ROWS = 16
COLS = 32


def shared_keys(key):
    return 1.7 * jax.random.normal(key, (FRAMES, ROWS, COLS, HEADS * HEAD_DIM), jnp.float32)


def draw_key_proj(key, part):
    base = shared_keys(key)
    return base.astype(jnp.bfloat16)


def draw_queries(key, part):
    key = jax.random.fold_in(key, 7)
    drawn = 1.7 * jax.random.normal(key, (FRAMES, ROWS, COLS, HEADS * HEAD_DIM), jnp.float32)
    return drawn.astype(jnp.bfloat16)


def shard_levels(own_key, extent, shards, smallest, largest):
    factor_of = 1.0
    for dim, parts in shards:
        heights = jax.random.uniform(jax.random.fold_in(jax.random.fold_in(own_key, 6), dim), (parts,), jnp.float32, smallest / len(shards), largest / len(shards))
        factor_of = factor_of * jnp.repeat(jnp.exp(heights), extent[dim] // parts).reshape((-1,) + (1,) * (len(extent) - 1 - dim))
    return factor_of


def noise(key, dims, deviation, most, shards=(), held_as=jnp.bfloat16):
    result = deviation * jax.random.normal(key, dims, jnp.float32)
    if shards:
        result = result * shard_levels(key, dims, shards, -0.22, 0.18)
    return jnp.clip(result, -most, most).astype(held_as)


def setup_inputs(seed: int = 0, part: int = 0) -> dict:
    key_of = jax.random.split(jax.random.key(seed), 15)
    own_keys = jax.random.split(jax.random.fold_in(key_of[14], part), 15)
    return {
        "queries": draw_queries(jax.random.fold_in(jax.random.fold_in(key_of[14], part), 71), part),
        "key_proj": draw_key_proj(jax.random.fold_in(jax.random.fold_in(key_of[14], part), 71), part),
        "values": noise(own_keys[2], (FRAMES, ROWS, COLS, HEADS * HEAD_DIM), 1.0, 6.0, ((1, 16), (2, 4))),
        "hidden_in": noise(own_keys[3], (FRAMES, ROWS, COLS, D), 0.5, 6.0, ((1, 16), (2, 4))),
        "out_weight": noise(key_of[4], (HEADS * HEAD_DIM, D), (HEADS * HEAD_DIM) ** -0.5, 0.09375, ((0, 16), (1, 4))),
        "out_gate": jnp.clip(1.0 + 0.18 * jax.random.normal(key_of[5], (D,), jnp.float32), 0.1, 1.9),
        "mod_shift": noise(key_of[6], (D,), 0.5, 3.0, (), jnp.float32),
        "mod_scale": jnp.clip(jax.random.uniform(key_of[7], (D,), jnp.float32, -0.5, 0.5), -0.5, 0.5),
        "head_weight": noise(key_of[8], (D, 4 * LAT_CH), D ** -0.5, 0.078125),
        "conv_first": noise(key_of[9], (27 * LAT_CH, VC), (27 * LAT_CH) ** -0.5, 0.3125),
        "bias_first": noise(key_of[10], (VC,), 0.5, 3.0, (), jnp.float32),
        "norm_gain": jnp.clip(1.0 + 0.18 * jax.random.normal(key_of[11], (VC,), jnp.float32), 0.1, 1.9),
        "conv_second": noise(key_of[12], (27 * VC, VC), (27 * VC) ** -0.5, 0.0625),
        "bias_second": noise(key_of[13], (VC,), 0.5, 3.0, (), jnp.float32),
    }


def head_attention(query_head, key_head, value_head, block_rows):
    blocks = query_head.reshape(-1, block_rows, query_head.shape[1])

    def one_block(block_queries):
        scores = jnp.einsum('qd,kd->qk', block_queries.astype(jnp.float32), key_head.astype(jnp.float32)) * HEAD_DIM ** (-0.5)
        row_max = lax.optimization_barrier(jnp.max(scores, axis=1, keepdims=True))
        expo_terms = jnp.exp(scores - row_max)
        totals = lax.optimization_barrier(jnp.sum(expo_terms, axis=1, keepdims=True))
        mixed = jnp.dot(expo_terms.astype(jnp.bfloat16), value_head, preferred_element_type=jnp.float32)
        return (mixed / totals).astype(jnp.bfloat16)
    return lax.map(one_block, blocks).reshape(-1, query_head.shape[1])

def causal_conv(padded, weight):
    frames = padded.shape[0] - 2
    height = padded.shape[1] - 2
    span_cols = padded.shape[2] - 2
    taps = [padded[t:t + frames, i:i + height, j:j + span_cols, :] for t in range(3) for i in range(3) for j in range(3)]
    stacked = jnp.concatenate(taps, axis=-1)
    flat_rows = stacked.reshape(-1, stacked.shape[-1])
    return jnp.dot(flat_rows, weight, preferred_element_type=jnp.float32).reshape(frames, height, span_cols, weight.shape[1])

def activate(first, norm_gain):
    wide = first.astype(jnp.float32)
    square_mean = lax.optimization_barrier(jnp.mean(wide * wide, axis=-1, keepdims=True))
    normed = wide * lax.rsqrt(square_mean + 1e-06) * norm_gain
    return jax.nn.silu(normed).astype(jnp.bfloat16)

def reference(queries, key_proj, values, hidden_in, out_weight, out_gate, mod_shift, mod_scale, head_weight, conv_first, bias_first, norm_gain, conv_second, bias_second):
    tokens = FRAMES * ROWS * COLS

    def split_heads(array):
        return array.reshape(tokens, HEADS, HEAD_DIM).transpose(1, 0, 2)

    def attend_one(operands):
        return head_attention(operands[0], operands[1], operands[2], ROWS * COLS)
    attended = lax.map(attend_one, (split_heads(queries), split_heads(key_proj), split_heads(values)))
    attended = attended.transpose(1, 0, 2).reshape(tokens, HEADS * HEAD_DIM)
    groups = HEADS // HEAD_DEV
    group_width = HEAD_DEV * HEAD_DIM
    grouped = attended.reshape(tokens, groups, group_width).transpose(1, 0, 2)
    stacked_weight = out_weight.reshape(groups, group_width, D)

    def add_group(total, operands):
        term = jnp.dot(operands[0], operands[1], preferred_element_type=jnp.float32)
        term = lax.optimization_barrier(term.astype(jnp.bfloat16)).astype(jnp.float32)
        return (total + term, None)
    projected, unused = lax.scan(add_group, jnp.zeros((tokens, D), jnp.float32), (grouped, stacked_weight))
    projected = projected.reshape(FRAMES, ROWS, COLS, D)
    block_out = (hidden_in.astype(jnp.float32) + out_gate * projected).astype(jnp.bfloat16)
    stream = block_out.astype(jnp.float32)
    row_mean = lax.optimization_barrier(jnp.mean(stream, axis=-1, keepdims=True))
    centred = stream - row_mean
    variance = lax.optimization_barrier(jnp.mean(centred * centred, axis=-1, keepdims=True))
    modded = (centred * lax.rsqrt(variance + 1e-06) * (1.0 + mod_scale) + mod_shift).astype(jnp.bfloat16)
    patch = jnp.dot(modded.reshape(-1, D), head_weight, preferred_element_type=jnp.float32).astype(jnp.bfloat16)
    patch = patch.reshape(FRAMES, ROWS, COLS, 2, 2, LAT_CH)
    latent = patch.transpose(0, 1, 3, 2, 4, 5).reshape(FRAMES, 2 * ROWS, 2 * COLS, LAT_CH)
    padding = ((2, 0), (1, 1), (1, 1), (0, 0))
    first = (causal_conv(jnp.pad(latent, padding), conv_first) + bias_first).astype(jnp.bfloat16)
    active = activate(first, norm_gain)
    second = causal_conv(jnp.pad(active, padding), conv_second)
    decoded = (first.astype(jnp.float32) + second + bias_second).astype(jnp.bfloat16)
    return (block_out, decoded)
```

```python
import jax
import jax.numpy as jnp
from jax import lax
from jax.experimental import pallas as pl
from jax.experimental.pallas import tpu as pltpu
from jax.sharding import Mesh, PartitionSpec as P

HEAD_DIM = 128
BF16 = jnp.bfloat16
F32 = jnp.float32
VMEM = pl.BlockSpec(memory_space=pltpu.VMEM)
HBM = pl.BlockSpec(memory_space=pltpu.HBM)


def in_hbm(array):
    return pltpu.with_memory_space_constraint(array, pltpu.HBM)


def call(kernel, out_shape, args, limit, bytes_accessed):
    return pl.pallas_call(
        kernel,
        out_shape=out_shape,
        in_specs=[VMEM] * len(args),
        out_specs=jax.tree.map(lambda _: VMEM, out_shape),
        compiler_params=pltpu.CompilerParams(vmem_limit_bytes=limit * 1024 * 1024),
        cost_estimate=pl.CostEstimate(flops=0, bytes_accessed=bytes_accessed, transcendentals=0),
    )(*args)


def pack_kernel(q_ref, k_ref, v_ref, w_ref, out_ref, low_ref, high_ref, inner_ref, held, packed, sems, out_sems):
    heads = out_ref.shape[0]
    step = w_ref.shape[0] // (sems.shape[0] - 3)
    copies = [
        pltpu.make_async_copy(ref, held.at[at], sems.at[at]) for at, ref in enumerate((q_ref, k_ref, v_ref))
    ]
    taken = 0
    for ref in (low_ref, high_ref, inner_ref):
        for row in range(0, ref.shape[0], step):
            source = w_ref.at[taken + row : taken + row + step]
            copies.append(pltpu.make_async_copy(source, ref.at[row : row + step], sems.at[len(copies)]))
        taken += ref.shape[0]
    for copy in copies:
        copy.start()
    sends = []
    for at in range(3):
        copies[at].wait()
        for h in range(heads):
            packed[at, h] = held[at, :, h * HEAD_DIM : (h + 1) * HEAD_DIM]
        place = out_ref.at[:, :, at * HEAD_DIM : (at + 1) * HEAD_DIM]
        sends.append(pltpu.make_async_copy(packed.at[at], place, out_sems.at[at]))
        sends[at].start()
    for copy in copies[3:] + sends:
        copy.wait()


FACTOR = HEAD_DIM ** (-0.5) * 1.4426950408889634


def scores_of(queries_ref, keys_ref, at):
    q = jnp.concatenate([queries_ref[2 * at + i, :, 0:HEAD_DIM] for i in range(2)], axis=0)
    k = keys_ref[:, :, HEAD_DIM : 2 * HEAD_DIM].reshape(-1, HEAD_DIM)
    return lax.dot_general(q, k, (((1,), (1,)), ((), ())), preferred_element_type=F32)


def own_attention_kernel(own_ref, mixed_ref, top_ref, total_ref):
    blocks = mixed_ref.shape[0]
    values = own_ref[:, :, 2 * HEAD_DIM : 3 * HEAD_DIM].reshape(-1, HEAD_DIM)
    following = scores_of(own_ref, own_ref, 0)
    for at in range(blocks):
        scores = following
        if at + 1 < blocks:
            following = scores_of(own_ref, own_ref, at + 1)
        top = jnp.max(scores, axis=1, keepdims=True)
        expo = jnp.exp2((scores - top) * FACTOR)
        top_ref[at] = top
        total_ref[at] = jnp.sum(expo, axis=1, keepdims=True)
        mixed_ref[at] = jnp.dot(expo.astype(BF16), values, preferred_element_type=F32)


def attention_kernel(own_ref, other_ref, mixed_ref, top_ref, total_ref, out_ref, result, sems):
    blocks, block, _ = mixed_ref.shape
    n_zl, copies, count, _ = out_ref.shape
    values = other_ref[:, :, 2 * HEAD_DIM : 3 * HEAD_DIM].reshape(-1, HEAD_DIM)
    sends = []
    following = scores_of(own_ref, other_ref, 0)
    for at in range(blocks):
        scores = following
        if at + 1 < blocks:
            following = scores_of(own_ref, other_ref, at + 1)
        top = jnp.maximum(top_ref[at], jnp.max(scores, axis=1, keepdims=True))
        expo = jnp.exp2((scores - top) * FACTOR)
        held = jnp.exp2((top_ref[at] - top) * FACTOR)
        total = total_ref[at] * held + jnp.sum(expo, axis=1, keepdims=True)
        mixed = mixed_ref[at] * held + jnp.dot(expo.astype(BF16), values, preferred_element_type=F32)
        result[at] = (mixed / total).astype(BF16)
        zl, start = at * block // count, at * block % count
        for copy in range(copies):
            place = out_ref.at[zl, copy, start : start + block]
            sends.append(pltpu.make_async_copy(result.at[at], place, sems.at[at, copy]))
            sends[-1].start()
    for send in sends:
        send.wait()


def projection_kernel(att_ref, *refs):
    refs, (out_ref, held, total, sems) = refs[:-4], refs[-4:]
    targets, rows, cols = out_ref.shape
    steps, depth, _ = held.shape
    n_x = att_ref.shape[0] // steps
    zl, core = lax.axis_index("zl"), lax.axis_index("core")
    starts = (0, refs[1].shape[0], refs[1].shape[0] + refs[2].shape[0])
    layout = ((0, 0), (1, starts[0]), (1, starts[1]), (1, starts[2]))
    copies = [[] for _ in range(steps)]
    for at, ref in enumerate(refs):
        step, start = layout[at % len(layout)]
        offset = (core if at < len(layout) else 1 - core) * (depth // 2)
        place = pl.ds(pl.multiple_of(offset + start, 16), ref.shape[0])
        copies[step].append(pltpu.make_async_copy(ref, held.at[step, place], sems.at[at]))
    for step in range(steps):
        for copy in copies[step]:
            copy.start()
    for step in range(steps):
        base = (zl if step == 0 else 1 - zl) * n_x
        feats = jnp.concatenate([att_ref[base + x] for x in range(n_x)], axis=1)
        for copy in copies[step]:
            copy.wait()
        term = jnp.dot(feats, held[step], preferred_element_type=F32)
        if step == 0:
            total[...] = term
        else:
            out_ref[...] = (total[...] + term).astype(BF16).reshape(targets, rows, cols)


def fetch_kernel(skip, after_ref, weight_ref, out_ref, sems):
    pieces = sems.shape[0]
    step = out_ref.shape[0] // pieces
    copies = [
        pltpu.make_async_copy(
            weight_ref.at[skip + at * step : skip + (at + 1) * step],
            out_ref.at[at * step : (at + 1) * step],
            sems.at[at],
        )
        for at in range(pieces)
    ]
    for copy in copies:
        copy.start()
    for copy in copies:
        copy.wait()


def fetch(weight, skip, rows, after):
    fetched = pl.pallas_call(
        lambda *refs: fetch_kernel(skip, *refs),
        out_shape=pltpu.VMEM((rows, weight.shape[1]), BF16),
        in_specs=[pl.BlockSpec(memory_space=pl.ANY), HBM],
        out_specs=VMEM,
        scratch_shapes=[pltpu.SemaphoreType.DMA((8,))],
        compiler_params=pltpu.CompilerParams(vmem_limit_bytes=8 * 1024 * 1024),
        cost_estimate=pl.CostEstimate(flops=0, bytes_accessed=4 * rows * weight.shape[1], transcendentals=0),
    )(after, in_hbm(weight))
    return pltpu.with_memory_space_constraint(fetched, pltpu.VMEM)


def head_kernel(splits, parts_ref, hidden_ref, gate_ref, shift_ref, scale_ref, head_ref, out_ref, patch_ref):
    quarters = parts_ref.shape[0] // splits
    tokens, cols = parts_ref.shape[1:]
    width = quarters * cols
    total = jnp.zeros((tokens, 1), F32)
    for quarter in range(quarters):
        span = slice(quarter * cols, (quarter + 1) * cols)
        acc = parts_ref[quarter].astype(F32)
        for split in range(1, splits):
            acc = acc + parts_ref[split * quarters + quarter].astype(F32)
        block_out = (hidden_ref[:, span].astype(F32) + gate_ref[:, span] * acc).astype(BF16)
        out_ref[:, span] = block_out
        total = total + jnp.sum(block_out.astype(F32), axis=1, keepdims=True)
    mean = total / width
    square = jnp.zeros((tokens, 1), F32)
    for quarter in range(quarters):
        span = slice(quarter * cols, (quarter + 1) * cols)
        centred = out_ref[:, span].astype(F32) - mean
        square = square + jnp.sum(centred * centred, axis=1, keepdims=True)
    inv = lax.rsqrt(square / width + 1e-06)
    patch = jnp.zeros((tokens, head_ref.shape[0]), F32)
    for quarter in range(quarters):
        span = slice(quarter * cols, (quarter + 1) * cols)
        centred = out_ref[:, span].astype(F32) - mean
        modded = (centred * inv * (1.0 + scale_ref[:, span]) + shift_ref[:, span]).astype(BF16)
        patch = patch + lax.dot_general(
            modded, head_ref[:, span], (((1,), (1,)), ((), ())), preferred_element_type=F32
        )
    patch_ref[...] = patch.astype(BF16).astype(F32)


def join_kernel(own_ref, left_ref, right_ref, after_ref, out_ref):
    col_at = lax.axis_index("tp")
    left = jnp.where(col_at == 0, 0.0, left_ref[...])
    right = jnp.where(col_at == 3, 0.0, right_ref[...])
    for f in range(out_ref.shape[0]):
        span = slice(8 * f, 8 * f + 8)
        out_ref[f, 0:8] = left[span]
        out_ref[f, 8:16] = own_ref[span]
        out_ref[f, 16:24] = right[span]


def decode_kernel(
    *refs,
):
    rows_in, refs = refs[:3], refs[3:]
    first_ref, bias1_ref, gain_ref, low_ref, high_ref, bias2_ref, out_ref, *refs = refs
    near, taps1, lhs1, first, active, lhs2, result = refs
    frames, cols = 4, 8
    lat = rows_in[0].shape[2] // 4
    chans = bias1_ref.shape[1]
    part = low_ref.shape[0]
    depth = (part + high_ref.shape[0]) // 3

    row_at = lax.axis_index(("zl", "y", "core"))
    col_at = lax.axis_index("tp")
    row_last, col_last = 15, 3
    near[...] = jnp.zeros_like(near)
    for r in range(3):
        row_out = (row_at == 0) if r == 0 else (row_at == row_last) if r == 2 else False
        rows = jnp.where(row_out, 0.0, rows_in[r][...])
        for f in range(frames):
            window = [rows[f, 7:15], rows[f, 8:16], rows[f, 9:17]]
            for a in range(2):
                span = slice(2 * lat * a, 2 * lat * (a + 1))
                row = jnp.concatenate(
                    [piece[:, span] for piece in window] + [jnp.zeros((cols, 128 - 6 * lat), F32)], axis=1
                )
                near[0, 2 + f, 2 * r + a] = row
                for v in range(1, 4):
                    near[v, 2 + f, 2 * r + a] = pltpu.roll(row, 128 - lat * v, 1)
    taps1[...] = jnp.zeros_like(taps1)
    for ti in range(9):
        taps1[128 * ti : 128 * ti + 3 * lat] = first_ref[3 * lat * ti : 3 * lat * (ti + 1)]
        t, i = ti // 3, ti % 3
        for v in range(4):
            piece = near[v, t : t + 4, i : i + 4].reshape(128, 128)
            lhs1[128 * v : 128 * (v + 1), 128 * ti : 128 * (ti + 1)] = piece.astype(BF16)

    col = lax.broadcasted_iota(jnp.int32, (frames, 4, cols, chans), 2)
    y = lax.broadcasted_iota(jnp.int32, (frames, 4, cols, chans), 1)
    outside_rows = ((y == 0) & (row_at == 0)) | ((y == 3) & (row_at == row_last))
    for v in range(4):
        value = jnp.dot(lhs1[128 * v : 128 * (v + 1)], taps1[...], preferred_element_type=F32) + bias1_ref[...]
        value = value.astype(BF16).astype(F32)
        if v in (1, 2):
            first[v - 1] = value.reshape(frames, 4, cols, chans)
        mean = jnp.mean(value * value, axis=1, keepdims=True)
        normed = value * lax.rsqrt(mean + 1e-06) * gain_ref[...]
        silu = (normed / (1.0 + jnp.exp(-normed))).reshape(frames, 4, cols, chans)
        outside = outside_rows
        if v == 0:
            outside = outside | ((col == 0) & (col_at == 0))
        if v == 3:
            outside = outside | ((col == cols - 1) & (col_at == col_last))
        active[:, :, v] = jnp.where(outside, 0.0, silu)

    for i in range(3):
        for j in range(3):
            piece = active[:, i : i + 2, j : j + 2].reshape(128, chans)
            at = chans * (3 * i + j)
            lhs2[:, at : at + chans] = piece.astype(BF16)
    total = jnp.zeros((128, chans), F32)
    for t in (2, 1, 0):
        rows = 32 * (2 + t)
        start, stop = depth * t, depth * (t + 1)
        term = jnp.zeros((rows, chans), F32)
        for ref, first_row in ((low_ref, 0), (high_ref, part)):
            low, high = max(start, first_row), min(stop, first_row + ref.shape[0])
            if low < high:
                weight = ref[low - first_row : high - first_row]
                term += jnp.dot(lhs2[0:rows, low - start : high - start], weight, preferred_element_type=F32)
        if t < 2:
            term = jnp.concatenate([jnp.zeros((128 - rows, chans), F32), term], axis=0)
        total = total + term
    total = (total + bias2_ref[...]).reshape(frames, 2, 2, cols, chans)
    for f in range(frames):
        for a in range(2):
            for b in range(2):
                cell = total[f, a, b] + first[b, f, 1 + a]
                for n in range(chans // 128):
                    result[n, f, a, pl.ds(b, cols, stride=2)] = cell[:, 128 * n : 128 * (n + 1)]
    for n in range(chans // 128):
        out_ref[:, :, :, 128 * n : 128 * (n + 1)] = result[n].astype(BF16)


def neighbours(block, axis):
    count = lax.axis_size(axis)
    forward = [(i, (i + 1) % count) for i in range(count)]
    backward = [(target, source) for source, target in forward]
    return lax.ppermute(block, axis, forward), lax.ppermute(block, axis, backward)


def shards(
    queries,
    key_proj,
    values,
    hidden_in,
    out_weight,
    out_gate,
    mod_shift,
    mod_scale,
    head_weight,
    conv_first,
    bias_first,
    norm_gain,
    conv_second,
    bias_second,
):
    frames, row_dev, col_dev, features = queries.shape
    width = hidden_in.shape[3]
    tokens = frames * row_dev * col_dev
    heads = features // HEAD_DIM
    n_zl, n_y, n_x, n_dp = (lax.axis_size(a) for a in ("zl", "y", "tp", "dp"))
    chips = n_zl * n_y * n_x
    assert heads == chips

    depth, n_cols = out_weight.shape
    weight_parts = [jax.ShapeDtypeStruct((rows, n_cols), BF16) for rows in (depth * 3 // 8, depth // 2, depth // 8)]
    packed, weight_low, weight_high, weight_inner = pl.pallas_call(
        pack_kernel,
        out_shape=(jax.ShapeDtypeStruct((heads, tokens, 3 * HEAD_DIM), BF16), *weight_parts),
        in_specs=[HBM] * 4,
        out_specs=(HBM, HBM, HBM, HBM),
        scratch_shapes=[
            pltpu.VMEM((3, tokens, features), BF16),
            pltpu.VMEM((3, heads, tokens, HEAD_DIM), BF16),
            pltpu.SemaphoreType.DMA((3 + 16,)),
            pltpu.SemaphoreType.DMA((3,)),
        ],
        compiler_params=pltpu.CompilerParams(vmem_limit_bytes=24 * 1024 * 1024),
    )(*[in_hbm(a.reshape(tokens, features)) for a in (queries, key_proj, values)], in_hbm(out_weight))
    own = lax.all_to_all(packed, ("zl", "y", "tp"), 0, 0, tiled=True)
    swap = [(0, 1), (1, 0)]
    outer = []
    for dp in range(n_dp):
        low, high = dp, n_dp + (dp - 1) % n_dp
        outer += [(low, high), (high, low)]
    from_first = lax.ppermute(weight_high, ("zl", "dp"), outer)
    from_inner = lax.ppermute(weight_inner, "zl", swap)
    own, from_first, from_inner = lax.optimization_barrier((own, from_first, from_inner))
    other = lax.ppermute(own, "core", swap)
    sources = (n_zl * n_y, n_x * tokens, 3 * HEAD_DIM)
    held = n_y * n_x * tokens
    blocks, block = n_zl * held // 256, 256
    stat = jax.ShapeDtypeStruct((blocks, block, 1), F32)
    own, other = own.reshape(sources), other.reshape(sources)
    mixed, top, total = call(
        own_attention_kernel,
        (jax.ShapeDtypeStruct((blocks, block, HEAD_DIM), F32), stat, stat),
        [own],
        limit=24,
        bytes_accessed=8 * 1024 * 1024,
    )
    attended_here = pl.pallas_call(
        attention_kernel,
        out_shape=jax.ShapeDtypeStruct((n_zl, n_x, held, HEAD_DIM), BF16),
        in_specs=[VMEM] * 5,
        out_specs=HBM,
        scratch_shapes=[
            pltpu.VMEM((blocks, block, HEAD_DIM), BF16),
            pltpu.SemaphoreType.DMA((blocks, n_x)),
        ],
        compiler_params=pltpu.CompilerParams(vmem_limit_bytes=24 * 1024 * 1024),
    )(own, other, mixed, top, total)
    attended = lax.all_to_all(
        attended_here.reshape(n_zl * n_x, held, HEAD_DIM), ("zl", "tp"), 0, 0, tiled=True
    )
    weight_low, out_weight, from_first, from_inner, _ = lax.optimization_barrier(
        (weight_low, out_weight, from_first, from_inner, attended_here)
    )
    from_last = lax.ppermute(weight_low, ("zl", "dp"), outer)
    near = (out_weight, from_last, from_first, from_inner)
    far = tuple(lax.ppermute(piece, "core", swap) for piece in near)
    terms = pl.pallas_call(
        projection_kernel,
        out_shape=jax.ShapeDtypeStruct((n_y * n_x, tokens, n_cols), BF16),
        in_specs=[VMEM] + [HBM] * 5 + [VMEM, HBM, HBM],
        out_specs=VMEM,
        scratch_shapes=[
            pltpu.VMEM((n_zl, 2 * out_weight.shape[0], n_cols), BF16),
            pltpu.VMEM((held, n_cols), F32),
            pltpu.SemaphoreType.DMA((8,)),
        ],
        compiler_params=pltpu.CompilerParams(vmem_limit_bytes=24 * 1024 * 1024),
    )(
        attended,
        *[in_hbm(piece) for piece in near + far[:1]],
        pltpu.with_memory_space_constraint(far[1], pltpu.VMEM),
        *[in_hbm(piece) for piece in far[2:]],
    )
    terms = lax.all_to_all(terms, ("y", "tp"), 0, 0, tiled=True)
    patch_width = head_weight.shape[1]
    block_out, patch = call(
        lambda *refs: head_kernel(n_y, *refs),
        (
            jax.ShapeDtypeStruct((tokens, width), BF16),
            jax.ShapeDtypeStruct((tokens, patch_width), F32),
        ),
        [
            terms,
            hidden_in.reshape(tokens, width),
            out_gate.reshape(1, width),
            mod_shift.reshape(1, width),
            mod_scale.reshape(1, width),
            head_weight.T,
        ],
        limit=12,
        bytes_accessed=16 * 1024 * 1024,
    )
    block_out = block_out.reshape(hidden_in.shape)

    left, right = neighbours(patch, "tp")
    part = conv_second.shape[0] // 256 * 128
    second_low = fetch(conv_second, 0, part, patch)
    joined = call(
        join_kernel,
        jax.ShapeDtypeStruct((frames, 24, patch_width), F32),
        [patch, left, right, second_low],
        limit=4,
        bytes_accessed=8 * 1024 * 1024,
    )
    above, below = neighbours(joined, ("zl", "y", "core"))
    second_high = fetch(conv_second, part, conv_second.shape[0] - part, joined)
    chans = conv_first.shape[1]
    depth = conv_second.shape[0] // 3
    decoded = pl.pallas_call(
        decode_kernel,
        out_shape=jax.ShapeDtypeStruct((frames, 2 * row_dev, 2 * col_dev, chans), BF16),
        in_specs=[VMEM] * 9,
        out_specs=VMEM,
        scratch_shapes=[
            pltpu.VMEM((4, frames + 2, 6, col_dev, 128), F32),
            pltpu.VMEM((9 * 128, chans), BF16),
            pltpu.VMEM((4 * 128, 9 * 128), BF16),
            pltpu.VMEM((2, frames, 4, col_dev, chans), F32),
            pltpu.VMEM((frames, 4, 4, col_dev, chans), F32),
            pltpu.VMEM((128, depth), BF16),
            pltpu.VMEM((chans // 128, frames, 2, 2 * col_dev, 128), F32),
        ],
        compiler_params=pltpu.CompilerParams(vmem_limit_bytes=32 * 1024 * 1024),
    )(
        above,
        joined,
        below,
        conv_first,
        bias_first.reshape(1, chans),
        norm_gain.reshape(1, chans),
        second_low,
        second_high,
        bias_second.reshape(1, chans),
    )
    return (block_out, decoded)


def solution(mesh):
    fine = Mesh(mesh.devices.reshape(2, 4, 2, *mesh.devices.shape[1:]), ("zl", "y", "core", "tp", "dp"))
    sp = ("zl", "y", "core")
    grid = P("dp", sp, "tp", None)
    in_specs = (grid, grid, grid, grid, P(sp, "tp")) + (P(),) * 9
    return jax.shard_map(
        shards, mesh=fine, in_specs=in_specs, out_specs=(grid, grid), check_vma=False
    )
```

```python
import jax
import jax.numpy as jnp
from jax import lax
from jax.experimental import pallas as pl
from jax.experimental.pallas import tpu as pltpu
from jax.sharding import Mesh, PartitionSpec as P

HEAD_DIM = 128
BF16 = jnp.bfloat16
F32 = jnp.float32
VMEM = pl.BlockSpec(memory_space=pltpu.VMEM)
HBM = pl.BlockSpec(memory_space=pltpu.HBM)


def in_hbm(array):
    return pltpu.with_memory_space_constraint(array, pltpu.HBM)


def call(kernel, out_shape, args, limit, bytes_accessed):
    return pl.pallas_call(
        kernel,
        out_shape=out_shape,
        in_specs=[VMEM] * len(args),
        out_specs=jax.tree.map(lambda _: VMEM, out_shape),
        compiler_params=pltpu.CompilerParams(vmem_limit_bytes=limit * 1024 * 1024),
        cost_estimate=pl.CostEstimate(flops=0, bytes_accessed=bytes_accessed, transcendentals=0),
    )(*args)


def pack_kernel(q_ref, k_ref, v_ref, w_ref, out_ref, low_ref, high_ref, held, packed, sems, out_sems):
    heads = out_ref.shape[0]
    split, depth = low_ref.shape[0], w_ref.shape[0]
    step = depth // (sems.shape[0] - 3)
    copies = [
        pltpu.make_async_copy(ref, held.at[at], sems.at[at]) for at, ref in enumerate((q_ref, k_ref, v_ref))
    ]
    for at, row in enumerate(range(0, depth, step)):
        target = low_ref.at[row : row + step] if row < split else high_ref.at[row - split : row - split + step]
        copies.append(pltpu.make_async_copy(w_ref.at[row : row + step], target, sems.at[3 + at]))
    for copy in copies:
        copy.start()
    sends = []
    for at in range(3):
        copies[at].wait()
        for h in range(heads):
            packed[at, h] = held[at, :, h * HEAD_DIM : (h + 1) * HEAD_DIM]
        place = out_ref.at[:, :, at * HEAD_DIM : (at + 1) * HEAD_DIM]
        sends.append(pltpu.make_async_copy(packed.at[at], place, out_sems.at[at]))
        sends[at].start()
    for copy in copies[3:] + sends:
        copy.wait()


FACTOR = HEAD_DIM ** (-0.5) * 1.4426950408889634


def scores_of(queries_ref, keys_ref, at):
    q = jnp.concatenate([queries_ref[2 * at + i, :, 0:HEAD_DIM] for i in range(2)], axis=0)
    k = keys_ref[:, :, HEAD_DIM : 2 * HEAD_DIM].reshape(-1, HEAD_DIM)
    return lax.dot_general(q, k, (((1,), (1,)), ((), ())), preferred_element_type=F32)


def own_attention_kernel(own_ref, mixed_ref, top_ref, total_ref):
    blocks = mixed_ref.shape[0]
    values = own_ref[:, :, 2 * HEAD_DIM : 3 * HEAD_DIM].reshape(-1, HEAD_DIM)
    following = scores_of(own_ref, own_ref, 0)
    for at in range(blocks):
        scores = following
        if at + 1 < blocks:
            following = scores_of(own_ref, own_ref, at + 1)
        top = jnp.max(scores, axis=1, keepdims=True)
        expo = jnp.exp2((scores - top) * FACTOR)
        top_ref[at] = top
        total_ref[at] = jnp.sum(expo, axis=1, keepdims=True)
        mixed_ref[at] = jnp.dot(expo.astype(BF16), values, preferred_element_type=F32)


def attention_kernel(own_ref, other_ref, mixed_ref, top_ref, total_ref, out_ref, result, sems):
    blocks, block, _ = mixed_ref.shape
    n_zl, copies, count, _ = out_ref.shape
    values = other_ref[:, :, 2 * HEAD_DIM : 3 * HEAD_DIM].reshape(-1, HEAD_DIM)
    sends = []
    following = scores_of(own_ref, other_ref, 0)
    for at in range(blocks):
        scores = following
        if at + 1 < blocks:
            following = scores_of(own_ref, other_ref, at + 1)
        top = jnp.maximum(top_ref[at], jnp.max(scores, axis=1, keepdims=True))
        expo = jnp.exp2((scores - top) * FACTOR)
        held = jnp.exp2((top_ref[at] - top) * FACTOR)
        total = total_ref[at] * held + jnp.sum(expo, axis=1, keepdims=True)
        mixed = mixed_ref[at] * held + jnp.dot(expo.astype(BF16), values, preferred_element_type=F32)
        result[at] = (mixed / total).astype(BF16)
        zl, start = at * block // count, at * block % count
        for copy in range(copies):
            place = out_ref.at[zl, copy, start : start + block]
            sends.append(pltpu.make_async_copy(result.at[at], place, sems.at[at, copy]))
            sends[-1].start()
    for send in sends:
        send.wait()


def projection_kernel(att_ref, *refs):
    refs, (out_ref, held, sems) = refs[:-3], refs[-3:]
    targets, rows, cols = out_ref.shape
    steps, depth, _ = held.shape
    n_x = att_ref.shape[0] // steps
    zl, core = lax.axis_index("zl"), lax.axis_index("core")
    layout = ((0, 0), (1, 0), (1, refs[1].shape[0]))
    copies = [[] for _ in range(steps)]
    for at, ref in enumerate(refs):
        step, start = layout[at % len(layout)]
        offset = (core if at < len(layout) else 1 - core) * (depth // 2)
        place = pl.ds(pl.multiple_of(offset + start, 16), ref.shape[0])
        copies[step].append(pltpu.make_async_copy(ref, held.at[step, place], sems.at[at]))
    for step in range(steps):
        for copy in copies[step]:
            copy.start()
    feats = jnp.concatenate(
        [att_ref[base + x] for base in (zl * n_x, (1 - zl) * n_x) for x in range(n_x)], axis=1
    )
    for step in range(steps):
        for copy in copies[step]:
            copy.wait()
    chunk = 256
    for start in range(0, cols, chunk):
        span = slice(start, start + chunk)
        weight = held[:, :, span].reshape(steps * depth, chunk)
        terms = jnp.dot(feats, weight, preferred_element_type=F32)
        out_ref[:, :, span] = terms.astype(BF16).reshape(targets, rows, chunk)


def fetch_kernel(skip, after_ref, weight_ref, out_ref, sems):
    pieces = sems.shape[0]
    step = out_ref.shape[0] // pieces
    copies = [
        pltpu.make_async_copy(
            weight_ref.at[skip + at * step : skip + (at + 1) * step],
            out_ref.at[at * step : (at + 1) * step],
            sems.at[at],
        )
        for at in range(pieces)
    ]
    for copy in copies:
        copy.start()
    for copy in copies:
        copy.wait()


def fetch(weight, skip, rows, after):
    fetched = pl.pallas_call(
        lambda *refs: fetch_kernel(skip, *refs),
        out_shape=pltpu.VMEM((rows, weight.shape[1]), BF16),
        in_specs=[pl.BlockSpec(memory_space=pl.ANY), HBM],
        out_specs=VMEM,
        scratch_shapes=[pltpu.SemaphoreType.DMA((4,))],
        compiler_params=pltpu.CompilerParams(vmem_limit_bytes=8 * 1024 * 1024),
        cost_estimate=pl.CostEstimate(flops=0, bytes_accessed=4 * rows * weight.shape[1], transcendentals=0),
    )(after, in_hbm(weight))
    return pltpu.with_memory_space_constraint(fetched, pltpu.VMEM)


def head_kernel(splits, parts_ref, hidden_ref, gate_ref, shift_ref, scale_ref, head_ref, out_ref, patch_ref):
    quarters = parts_ref.shape[0] // splits
    tokens, cols = parts_ref.shape[1:]
    width = quarters * cols
    total = jnp.zeros((tokens, 1), F32)
    for quarter in range(quarters):
        span = slice(quarter * cols, (quarter + 1) * cols)
        acc = parts_ref[quarter].astype(F32)
        for split in range(1, splits):
            acc = acc + parts_ref[split * quarters + quarter].astype(F32)
        block_out = (hidden_ref[:, span].astype(F32) + gate_ref[:, span] * acc).astype(BF16)
        out_ref[:, span] = block_out
        total = total + jnp.sum(block_out.astype(F32), axis=1, keepdims=True)
    mean = total / width
    square = jnp.zeros((tokens, 1), F32)
    for quarter in range(quarters):
        span = slice(quarter * cols, (quarter + 1) * cols)
        centred = out_ref[:, span].astype(F32) - mean
        square = square + jnp.sum(centred * centred, axis=1, keepdims=True)
    inv = lax.rsqrt(square / width + 1e-06)
    patch = jnp.zeros((tokens, head_ref.shape[0]), F32)
    for quarter in range(quarters):
        span = slice(quarter * cols, (quarter + 1) * cols)
        centred = out_ref[:, span].astype(F32) - mean
        modded = (centred * inv * (1.0 + scale_ref[:, span]) + shift_ref[:, span]).astype(BF16)
        patch = patch + lax.dot_general(
            modded, head_ref[:, span], (((1,), (1,)), ((), ())), preferred_element_type=F32
        )
    patch_ref[...] = patch.astype(BF16).astype(F32)


def join_kernel(own_ref, left_ref, right_ref, after_ref, out_ref):
    col_at = lax.axis_index("tp")
    left = jnp.where(col_at == 0, 0.0, left_ref[...])
    right = jnp.where(col_at == 3, 0.0, right_ref[...])
    for f in range(out_ref.shape[0]):
        span = slice(8 * f, 8 * f + 8)
        out_ref[f, 0:8] = left[span]
        out_ref[f, 8:16] = own_ref[span]
        out_ref[f, 16:24] = right[span]


def decode_kernel(
    *refs,
):
    rows_in, refs = refs[:3], refs[3:]
    first_ref, bias1_ref, gain_ref, low_ref, high_ref, bias2_ref, out_ref, *refs = refs
    near, taps1, lhs1, first, active, lhs2, result = refs
    frames, cols = 4, 8
    lat = rows_in[0].shape[2] // 4
    chans = bias1_ref.shape[1]
    part = low_ref.shape[0]
    depth = (part + high_ref.shape[0]) // 3

    row_at = lax.axis_index(("zl", "y", "core"))
    col_at = lax.axis_index("tp")
    row_last, col_last = 15, 3
    near[...] = jnp.zeros_like(near)
    for r in range(3):
        row_out = (row_at == 0) if r == 0 else (row_at == row_last) if r == 2 else False
        rows = jnp.where(row_out, 0.0, rows_in[r][...])
        for f in range(frames):
            window = [rows[f, 7:15], rows[f, 8:16], rows[f, 9:17]]
            for a in range(2):
                span = slice(2 * lat * a, 2 * lat * (a + 1))
                row = jnp.concatenate(
                    [piece[:, span] for piece in window] + [jnp.zeros((cols, 128 - 6 * lat), F32)], axis=1
                )
                near[0, 2 + f, 2 * r + a] = row
                for v in range(1, 4):
                    near[v, 2 + f, 2 * r + a] = pltpu.roll(row, 128 - lat * v, 1)
    taps1[...] = jnp.zeros_like(taps1)
    for ti in range(9):
        taps1[128 * ti : 128 * ti + 3 * lat] = first_ref[3 * lat * ti : 3 * lat * (ti + 1)]
        t, i = ti // 3, ti % 3
        for v in range(4):
            piece = near[v, t : t + 4, i : i + 4].reshape(128, 128)
            lhs1[128 * v : 128 * (v + 1), 128 * ti : 128 * (ti + 1)] = piece.astype(BF16)

    col = lax.broadcasted_iota(jnp.int32, (frames, 4, cols, chans), 2)
    y = lax.broadcasted_iota(jnp.int32, (frames, 4, cols, chans), 1)
    outside_rows = ((y == 0) & (row_at == 0)) | ((y == 3) & (row_at == row_last))
    for v in range(4):
        value = jnp.dot(lhs1[128 * v : 128 * (v + 1)], taps1[...], preferred_element_type=F32) + bias1_ref[...]
        value = value.astype(BF16).astype(F32)
        if v in (1, 2):
            first[v - 1] = value.reshape(frames, 4, cols, chans)
        mean = jnp.mean(value * value, axis=1, keepdims=True)
        normed = value * lax.rsqrt(mean + 1e-06) * gain_ref[...]
        silu = (normed / (1.0 + jnp.exp(-normed))).reshape(frames, 4, cols, chans)
        outside = outside_rows
        if v == 0:
            outside = outside | ((col == 0) & (col_at == 0))
        if v == 3:
            outside = outside | ((col == cols - 1) & (col_at == col_last))
        active[:, :, v] = jnp.where(outside, 0.0, silu)

    for i in range(3):
        for j in range(3):
            piece = active[:, i : i + 2, j : j + 2].reshape(128, chans)
            at = chans * (3 * i + j)
            lhs2[:, at : at + chans] = piece.astype(BF16)
    total = jnp.zeros((128, chans), F32)
    for t in (2, 1, 0):
        rows = 32 * (2 + t)
        start, stop = depth * t, depth * (t + 1)
        term = jnp.zeros((rows, chans), F32)
        for ref, first_row in ((low_ref, 0), (high_ref, part)):
            low, high = max(start, first_row), min(stop, first_row + ref.shape[0])
            if low < high:
                weight = ref[low - first_row : high - first_row]
                term += jnp.dot(lhs2[0:rows, low - start : high - start], weight, preferred_element_type=F32)
        if t < 2:
            term = jnp.concatenate([jnp.zeros((128 - rows, chans), F32), term], axis=0)
        total = total + term
    total = (total + bias2_ref[...]).reshape(frames, 2, 2, cols, chans)
    for f in range(frames):
        for a in range(2):
            for b in range(2):
                cell = total[f, a, b] + first[b, f, 1 + a]
                for c in range(cols):
                    result[f, a, 2 * c + b : 2 * c + b + 1] = cell[c : c + 1]
    out_ref[...] = result[...].astype(BF16)


def neighbours(block, axis):
    count = lax.axis_size(axis)
    forward = [(i, (i + 1) % count) for i in range(count)]
    backward = [(target, source) for source, target in forward]
    return lax.ppermute(block, axis, forward), lax.ppermute(block, axis, backward)


def shards(
    queries,
    key_proj,
    values,
    hidden_in,
    out_weight,
    out_gate,
    mod_shift,
    mod_scale,
    head_weight,
    conv_first,
    bias_first,
    norm_gain,
    conv_second,
    bias_second,
):
    frames, row_dev, col_dev, features = queries.shape
    width = hidden_in.shape[3]
    tokens = frames * row_dev * col_dev
    heads = features // HEAD_DIM
    n_zl, n_y, n_x, n_dp = (lax.axis_size(a) for a in ("zl", "y", "tp", "dp"))
    chips = n_zl * n_y * n_x
    assert heads == chips

    depth, n_cols = out_weight.shape
    weight_parts = [jax.ShapeDtypeStruct((rows, n_cols), BF16) for rows in (depth * 7 // 16, depth * 9 // 16)]
    packed, weight_low, weight_high = pl.pallas_call(
        pack_kernel,
        out_shape=(jax.ShapeDtypeStruct((heads, tokens, 3 * HEAD_DIM), BF16), *weight_parts),
        in_specs=[HBM] * 4,
        out_specs=(HBM, HBM, HBM),
        scratch_shapes=[
            pltpu.VMEM((3, tokens, features), BF16),
            pltpu.VMEM((3, heads, tokens, HEAD_DIM), BF16),
            pltpu.SemaphoreType.DMA((3 + 16,)),
            pltpu.SemaphoreType.DMA((3,)),
        ],
        compiler_params=pltpu.CompilerParams(vmem_limit_bytes=24 * 1024 * 1024),
    )(*[in_hbm(a.reshape(tokens, features)) for a in (queries, key_proj, values)], in_hbm(out_weight))
    own = lax.all_to_all(packed, ("zl", "y", "tp"), 0, 0, tiled=True)
    swap = [(0, 1), (1, 0)]
    outer = []
    for dp in range(n_dp):
        low, high = dp, n_dp + (dp - 1) % n_dp
        outer += [(low, high), (high, low)]
    from_first = lax.ppermute(weight_high, ("zl", "dp"), outer)
    own, from_first = lax.optimization_barrier((own, from_first))
    other = lax.ppermute(own, "core", swap)
    sources = (n_zl * n_y, n_x * tokens, 3 * HEAD_DIM)
    held = n_y * n_x * tokens
    blocks, block = n_zl * held // 256, 256
    stat = jax.ShapeDtypeStruct((blocks, block, 1), F32)
    own, other = own.reshape(sources), other.reshape(sources)
    mixed, top, total = call(
        own_attention_kernel,
        (jax.ShapeDtypeStruct((blocks, block, HEAD_DIM), F32), stat, stat),
        [own],
        limit=24,
        bytes_accessed=8 * 1024 * 1024,
    )
    attended_here = pl.pallas_call(
        attention_kernel,
        out_shape=jax.ShapeDtypeStruct((n_zl, n_x, held, HEAD_DIM), BF16),
        in_specs=[VMEM] * 5,
        out_specs=HBM,
        scratch_shapes=[
            pltpu.VMEM((blocks, block, HEAD_DIM), BF16),
            pltpu.SemaphoreType.DMA((blocks, n_x)),
        ],
        compiler_params=pltpu.CompilerParams(vmem_limit_bytes=24 * 1024 * 1024),
    )(own, other, mixed, top, total)
    attended = lax.all_to_all(
        attended_here.reshape(n_zl * n_x, held, HEAD_DIM), ("zl", "tp"), 0, 0, tiled=True
    )
    weight_low, out_weight, from_first, _ = lax.optimization_barrier(
        (weight_low, out_weight, from_first, attended_here)
    )
    from_last = lax.ppermute(weight_low, ("zl", "dp"), outer)
    near = (out_weight, from_last, from_first)
    far = tuple(lax.ppermute(piece, "core", swap) for piece in near)
    terms = pl.pallas_call(
        projection_kernel,
        out_shape=jax.ShapeDtypeStruct((n_y * n_x, tokens, n_cols), BF16),
        in_specs=[VMEM] + [HBM] * 6,
        out_specs=VMEM,
        scratch_shapes=[
            pltpu.VMEM((n_zl, 2 * out_weight.shape[0], n_cols), BF16),
            pltpu.SemaphoreType.DMA((6,)),
        ],
        compiler_params=pltpu.CompilerParams(vmem_limit_bytes=24 * 1024 * 1024),
    )(attended, *[in_hbm(piece) for piece in near + far])
    terms = lax.all_to_all(terms, ("y", "tp"), 0, 0, tiled=True)
    patch_width = head_weight.shape[1]
    block_out, patch = call(
        lambda *refs: head_kernel(n_y, *refs),
        (
            jax.ShapeDtypeStruct((tokens, width), BF16),
            jax.ShapeDtypeStruct((tokens, patch_width), F32),
        ),
        [
            terms,
            hidden_in.reshape(tokens, width),
            out_gate.reshape(1, width),
            mod_shift.reshape(1, width),
            mod_scale.reshape(1, width),
            head_weight.T,
        ],
        limit=12,
        bytes_accessed=16 * 1024 * 1024,
    )
    block_out = block_out.reshape(hidden_in.shape)

    left, right = neighbours(patch, "tp")
    part = conv_second.shape[0] // 256 * 128
    second_low = fetch(conv_second, 0, part, patch)
    joined = call(
        join_kernel,
        jax.ShapeDtypeStruct((frames, 24, patch_width), F32),
        [patch, left, right, second_low],
        limit=4,
        bytes_accessed=8 * 1024 * 1024,
    )
    above, below = neighbours(joined, ("zl", "y", "core"))
    second_high = fetch(conv_second, part, conv_second.shape[0] - part, joined)
    chans = conv_first.shape[1]
    depth = conv_second.shape[0] // 3
    decoded = pl.pallas_call(
        decode_kernel,
        out_shape=jax.ShapeDtypeStruct((frames, 2 * row_dev, 2 * col_dev, chans), BF16),
        in_specs=[VMEM] * 9,
        out_specs=VMEM,
        scratch_shapes=[
            pltpu.VMEM((4, frames + 2, 6, col_dev, 128), F32),
            pltpu.VMEM((9 * 128, chans), BF16),
            pltpu.VMEM((4 * 128, 9 * 128), BF16),
            pltpu.VMEM((2, frames, 4, col_dev, chans), F32),
            pltpu.VMEM((frames, 4, 4, col_dev, chans), F32),
            pltpu.VMEM((128, depth), BF16),
            pltpu.VMEM((frames, 2, 2 * col_dev, chans), F32),
        ],
        compiler_params=pltpu.CompilerParams(vmem_limit_bytes=32 * 1024 * 1024),
    )(
        above,
        joined,
        below,
        conv_first,
        bias_first.reshape(1, chans),
        norm_gain.reshape(1, chans),
        second_low,
        second_high,
        bias_second.reshape(1, chans),
    )
    return (block_out, decoded)


def solution(mesh):
    fine = Mesh(mesh.devices.reshape(2, 4, 2, *mesh.devices.shape[1:]), ("zl", "y", "core", "tp", "dp"))
    sp = ("zl", "y", "core")
    grid = P("dp", sp, "tp", None)
    in_specs = (grid, grid, grid, grid, P(sp, "tp")) + (P(),) * 9
    return jax.shard_map(
        shards, mesh=fine, in_specs=in_specs, out_specs=(grid, grid), check_vma=False
    )
```
